32 devices in a mesh: tok: 4 (over x, core), hid: 8 (over z, y).
Axes of the slice: x: 2, y: 2, z: 4, core: 2. Of those that a mesh axis runs over, the one named last changes fastest.
Arguments:
- gate_pre: bfloat16 [512, 24576], P('tok', 'hid'), may hold values from -6 to 6
- up_pre: bfloat16 [512, 24576], P('tok', 'hid'), may hold values from -6 to 6
- down_weight: bfloat16 [24576, 6144], P('hid', 'tok'), may hold values from -0.0546875 to 0.0546875
- residual: bfloat16 [512, 6144], P('tok', 'hid'), may hold values from -3 to 3
Outputs:
- mixed: bfloat16 [512, 6144], P('tok', 'hid')
The draws below stay inside these ranges and needn't reach their ends.
All inputs are finite; a program needn't handle non-finite values.
Results may differ from the reference program's by a relative error of at most 0.0043.
Values may be sent and summed in bfloat16 or wider, within the bound.
A program may use at most 64 MiB of HBM per device.

```python
import jax
import jax.numpy as jnp

D = 6144
FF = 24576
TOKENS = 512


def strengthened(array, rng, source, target, parts, factor):
    owner, partner = [(jnp.arange(array.shape[dim]) // (array.shape[dim] // parts)).reshape([-1 if axis == dim else 1 for axis in range(array.ndim)]) for dim in (source, target)]
    chosen = jax.random.permutation(rng, parts)[partner]
    strong = (owner == chosen) | (owner == (partner + parts // 2) % parts)
    return jnp.where(strong, factor * array, array)


def level_of(rng, shape, shards, low, top_value):
    loudness = 1.0
    for dim, parts in shards:
        heights = jax.random.uniform(jax.random.fold_in(jax.random.fold_in(rng, 6), dim), (parts,), jnp.float32, low / len(shards), top_value / len(shards))
        loudness = loudness * jnp.repeat(jnp.exp(heights), shape[dim] // parts).reshape((-1,) + (1,) * (len(shape) - 1 - dim))
    return loudness


def bell_draw(key, extent, deviation, most, shards=(), held_as=jnp.bfloat16):
    array = jax.random.normal(key, extent, jnp.float32) * deviation
    if len(shards) > 0:
        array = level_of(key, extent, shards, -0.22, 0.18) * array
    return jnp.clip(array, min=-most, max=most).astype(held_as)


def bell_draw_with(rng, shape, spread, most, cuts, heavy, held_as=jnp.bfloat16):
    values = spread * jax.random.normal(rng, shape, jnp.float32)
    if cuts:
        values = values * level_of(rng, shape, cuts, -0.22, 0.18)
    return jnp.clip(strengthened(values, jax.random.fold_in(rng, 3), *heavy), -most, most).astype(held_as)


def setup_inputs(seed: int = 0) -> dict:
    keys = jax.random.split(jax.random.key(seed), 5)
    return {
        "gate_pre": bell_draw(keys[0], (TOKENS, FF), 1.0, 6.0, ((0, 4), (1, 8))),
        "up_pre": bell_draw(keys[1], (TOKENS, FF), 1.0, 6.0, ((0, 4), (1, 8))),
        "down_weight": bell_draw_with(keys[2], (FF, D), FF ** -0.5, 0.0546875, ((0, 8), (1, 4)), (0, 1, 8, 2.0)),
        "residual": bell_draw(keys[3], (TOKENS, D), 0.5, 3.0, ((0, 4), (1, 8))),
    }


def reference(gate_pre, up_pre, down_weight, residual):
    hidden = (jax.nn.silu(gate_pre.astype(jnp.float32)) * up_pre.astype(jnp.float32)).astype(jnp.bfloat16)
    summed = jnp.dot(hidden, down_weight, preferred_element_type=jnp.float32)
    return (summed + residual.astype(jnp.float32)).astype(jnp.bfloat16)
```

```python
import jax
import jax.numpy as jnp
from jax import lax
from jax.experimental import pallas as pl
from jax.experimental.pallas import tpu as pltpu
from jax.sharding import PartitionSpec as P

MESH = pl.DeviceIdType.MESH
ROWS = 32
TILE = 256
F32, BF16 = jnp.float32, jnp.bfloat16


def collective_form(gate_pre, up_pre, down_weight, residual):
    hidden = (jax.nn.silu(gate_pre.astype(F32)) * up_pre.astype(F32)).astype(BF16)
    every_token = jnp.dot(
        lax.all_gather(hidden, "tok", axis=0, tiled=True),
        down_weight,
        preferred_element_type=F32,
    )
    partial_value = lax.all_to_all(every_token, "tok", split_axis=0, concat_axis=1, tiled=True)
    summed = lax.psum_scatter(partial_value, "hid", scatter_dimension=1, tiled=True)
    return (summed + residual.astype(F32)).astype(BF16)


def kernel(
    gate, up, weight, out,
    gbuf, ubuf, wbuf, hbuf, acc, ysend, yrecv, zsend, zrecv, fsend, land,
    gsem, usem, wsem, xs, xr, cs, cr, ls, lr, ys, yr, zs, zr, fs, fr,
):
    nk, rows, ff = gbuf.shape
    ng, _, half = acc.shape
    t, h = lax.axis_index("tok"), lax.axis_index("hid")
    x, c = lax.div(t, 2), lax.rem(t, 2)
    z, y = lax.div(h, 2), lax.rem(h, 2)
    z1, z0 = lax.div(z, 2), lax.rem(z, 2)
    gathers = z0 == c
    core_t, x_t = 2 * x + 1 - c, 2 * (1 - x) + c
    y_h, z_h = 2 * z + 1 - y, 2 * (2 * z1 + 1 - z0) + y

    def load(k, source, buf, sem):
        return pltpu.make_async_copy(source.at[pl.ds(k * rows, rows)], buf.at[k], sem.at[k])

    def load_weight(which):
        columns = pl.ds(pl.multiple_of((1 - y if which == 0 else y) * half, 128), half)
        return pltpu.make_async_copy(weight.at[:, columns], wbuf.at[which], wsem.at[which])

    def remote(src, dst, send, recv, tok, hid):
        return pltpu.make_async_remote_copy(
            src_ref=src, dst_ref=dst, send_sem=send, recv_sem=recv,
            device_id=(tok, hid), device_id_type=MESH,
        )

    def block(g, core):
        return hbuf.at[g, pl.ds(pl.multiple_of(core * rows, rows), rows)]

    def core_copy(k, core):
        return remote(block(k, core), block(k, core), cs.at[k], cr.at[k], core_t, h)

    def x_copy(k):
        return remote(block(k, c), block(nk + k, c), xs.at[k], xr.at[k], x_t, h)

    def relay(k, core):
        return remote(block(nk + k, core), block(nk + k, core), ls.at[k], lr.at[k], core_t, h)

    def y_copy(g):
        return remote(ysend.at[g], yrecv.at[g], ys.at[g], yr.at[g], t, y_h)

    def z_copy(g):
        return remote(zsend.at[g], zrecv.at[g], zs.at[g], zr.at[g], t, z_h)

    def final_copy(g, core, slot, k, tok):
        return remote(
            fsend.at[g, pl.ds(core * rows, rows)], land.at[slot, k],
            fs.at[g, core], fr.at[slot, k], tok, 2 * t + y,
        )

    for k in range(nk):
        load(k, gate, gbuf, gsem).start()
        load(k, up, ubuf, usem).start()
    load_weight(0).start()
    load_weight(1).start()

    barrier = pltpu.get_barrier_semaphore()

    def greet(tok, hid):
        pl.semaphore_signal(barrier, inc=1, device_id=(tok, hid), device_id_type=MESH)

    greet(core_t, h)
    greet(x_t, h)
    greet(t, y_h)

    @pl.when(gathers)
    def _():
        greet(t, z_h)

    source_h = [2 * (2 * slot + lax.rem(z, 2)) + y for slot in range(2)]
    local_land = [jnp.logical_and(z == t, z1 == slot) for slot in range(2)]
    for slot in range(2):

        @pl.when(jnp.logical_not(local_land[slot]))
        def _():
            greet(z, source_h[slot])

    owners = jnp.where(z == t, 3, 4)
    pl.semaphore_wait(barrier, 3 + jnp.where(gathers, owners, 1))

    wide = 512

    def activate(k, _):
        load(k, gate, gbuf, gsem).wait()
        load(k, up, ubuf, usem).wait()

        def piece(j, _):
            columns = pl.ds(pl.multiple_of(j * wide, wide), wide)
            v = gbuf[k, :, columns].astype(F32)
            u = ubuf[k, :, columns].astype(F32)
            block(k, c)[:, columns] = (v / (1.0 + jnp.exp(-v)) * u).astype(BF16)
            return 0

        lax.fori_loop(0, ff // wide, piece, 0)
        x_copy(k).start()
        core_copy(k, c).start()
        return 0

    lax.fori_loop(0, nk, activate, 0)

    def tiles(step):
        def one(n, _):
            step(pl.ds(pl.multiple_of(n * TILE, TILE), TILE))
            return 0

        lax.fori_loop(0, half // TILE, one, 0)

    def after_y(g):
        y_copy(g).wait_recv()

        @pl.when(gathers)
        def _():
            def step(cols):
                acc[g, :, cols] = acc[g, :, cols] + yrecv[g, :, cols].astype(F32)

            tiles(step)

        @pl.when(jnp.logical_not(gathers))
        def _():
            def step(cols):
                zsend[g, :, cols] = (acc[g, :, cols] + yrecv[g, :, cols].astype(F32)).astype(BF16)

            tiles(step)
            z_copy(g).start()

    def owner_of(g, core):
        chip = jnp.where(g < nk, x, 1 - x)
        tok = 2 * chip + core
        return tok, lax.rem(g, nk), jnp.logical_and(tok == t, z == t)

    def after_z(g):
        @pl.when(gathers)
        def _():
            z_copy(g).wait_recv()

            def step(cols):
                fsend[g, :, cols] = (acc[g, :, cols] + zrecv[g, :, cols].astype(F32)).astype(BF16)

            tiles(step)
            for core in range(2):
                tok, k, local = owner_of(g, core)

                @pl.when(local)
                def _():
                    land[z1, k] = fsend[g, core * rows : (core + 1) * rows]

                @pl.when(jnp.logical_not(local))
                def _():
                    final_copy(g, core, z1, k, tok).start()

    def chunk(g, _):
        @pl.when(jnp.logical_and(g >= nk, g < ng))
        def _():
            x_copy(g - nk).wait_recv()
            relay(g - nk, c).start()

        @pl.when(jnp.logical_and(g >= 1, g <= ng))
        def _():
            after_y(g - 1)

        @pl.when(g >= 2)
        def _():
            after_z(g - 2)

        @pl.when(g < ng)
        def _():
            @pl.when(g < nk)
            def _():
                core_copy(g, 1 - c).wait_recv()

            @pl.when(g >= nk)
            def _():
                relay(g - nk, 1 - c).wait_recv()

            def product(which, cols):
                return jnp.dot(hbuf[g], wbuf[which, :, cols], preferred_element_type=F32)

            @pl.when(g == 0)
            def _():
                load_weight(0).wait()

            def give(cols):
                ysend[g, :, cols] = product(0, cols).astype(BF16)

            tiles(give)
            y_copy(g).start()

            @pl.when(g == 0)
            def _():
                load_weight(1).wait()

            def keep(cols):
                acc[g, :, cols] = product(1, cols)

            tiles(keep)

        return 0

    lax.fori_loop(0, ng + 2, chunk, 0)

    def finish(k, _):
        for slot in range(2):

            @pl.when(jnp.logical_not(local_land[slot]))
            def _():
                final_copy(0, 0, slot, k, core_t).wait_recv()

        span = pl.ds(pl.multiple_of(k * rows, rows), rows)
        out[span, :] = land[0, k].astype(F32) + land[1, k].astype(F32)
        return 0

    lax.fori_loop(0, nk, finish, 0)

    def drain_k(k, _):
        x_copy(k).wait_send()
        core_copy(k, c).wait_send()
        relay(k, c).wait_send()
        return 0

    lax.fori_loop(0, nk, drain_k, 0)

    def drain_g(g, _):
        y_copy(g).wait_send()

        @pl.when(jnp.logical_not(gathers))
        def _():
            z_copy(g).wait_send()

        @pl.when(gathers)
        def _():
            for core in range(2):
                tok, k, local = owner_of(g, core)

                @pl.when(jnp.logical_not(local))
                def _():
                    final_copy(g, core, z1, k, tok).wait_send()

        return 0

    lax.fori_loop(0, ng, drain_g, 0)


def kernel_form(gate_pre, up_pre, down_weight, residual):
    tokens, ff = gate_pre.shape
    half = residual.shape[1]
    rows = ROWS
    nk = tokens // rows
    ng = 2 * nk
    dma = pltpu.SemaphoreType.DMA
    summed = pl.pallas_call(
        kernel,
        out_shape=jax.ShapeDtypeStruct((tokens, half), F32),
        in_specs=[pl.BlockSpec(memory_space=pl.ANY)] * 3,
        out_specs=pl.BlockSpec(memory_space=pltpu.VMEM),
        scratch_shapes=[
            pltpu.VMEM((nk, rows, ff), BF16),
            pltpu.VMEM((nk, rows, ff), BF16),
            pltpu.VMEM((2, ff, half), BF16),
            pltpu.VMEM((ng, 2 * rows, ff), BF16),
            pltpu.VMEM((ng, 2 * rows, half), F32),
        ]
        + [pltpu.VMEM((ng, 2 * rows, half), BF16)] * 5
        + [pltpu.VMEM((2, nk, rows, half), BF16)]
        + [dma((nk,)), dma((nk,)), dma((2,))]
        + [dma((nk,))] * 6
        + [dma((ng,))] * 4
        + [dma((ng, 2)), dma((2, nk))],
        compiler_params=pltpu.CompilerParams(
            collective_id=0, has_side_effects=True, vmem_limit_bytes=50 * 2**20
        ),
        cost_estimate=pl.CostEstimate(
            flops=2 * 4 * tokens * ff * 2 * half,
            bytes_accessed=2 * ff * (2 * half + 2 * tokens),
            transcendentals=tokens * ff,
        ),
    )(gate_pre, up_pre, down_weight)
    return (summed + residual.astype(F32)).astype(BF16)


def solution(mesh):
    in_specs = (P("tok", "hid"), P("tok", "hid"), P("hid", "tok"), P("tok", "hid"))
    out_specs = P("tok", "hid")
    fits = mesh.shape["tok"] == 4 and mesh.shape["hid"] == 8
    return jax.shard_map(
        kernel_form if fits else collective_form,
        mesh=mesh, in_specs=in_specs, out_specs=out_specs, check_vma=False,
    )
```

```python
import jax
import jax.numpy as jnp
from jax import lax
from jax.experimental import pallas as pl
from jax.experimental.pallas import tpu as pltpu
from jax.sharding import PartitionSpec as P

MESH = pl.DeviceIdType.MESH
ROWS = 32
TILE = 256
F32, BF16 = jnp.float32, jnp.bfloat16


def collective_form(gate_pre, up_pre, down_weight, residual):
    hidden = (jax.nn.silu(gate_pre.astype(F32)) * up_pre.astype(F32)).astype(BF16)
    every_token = jnp.dot(
        lax.all_gather(hidden, "tok", axis=0, tiled=True),
        down_weight,
        preferred_element_type=F32,
    )
    partial_value = lax.all_to_all(every_token, "tok", split_axis=0, concat_axis=1, tiled=True)
    summed = lax.psum_scatter(partial_value, "hid", scatter_dimension=1, tiled=True)
    return (summed + residual.astype(F32)).astype(BF16)


def kernel(
    gate, up, weight, out,
    gbuf, ubuf, wbuf, hown, hrem,
    acc_o, ysend_o, yrecv_o, zsend_o, zrecv_o, fsend_o,
    acc_r, ysend_r, yrecv_r, zsend_r, zrecv_r, fsend_r, land,
    gsem, usem, wsem, xs, xr, cs, cr, ls, lr, ys, yr, zs, zr, fs, fr,
):
    nk, rows, ff = gbuf.shape
    nt, _, tile = acc_o.shape
    half, tokens = nt * tile, nk * rows
    t, h = lax.axis_index("tok"), lax.axis_index("hid")
    x, c = lax.div(t, 2), lax.rem(t, 2)
    z, y = lax.div(h, 2), lax.rem(h, 2)
    z1, z0 = lax.div(z, 2), lax.rem(z, 2)
    gathers = z0 == c
    passes = jnp.logical_not(gathers)
    core_t, x_t = 2 * x + 1 - c, 2 * (1 - x) + c
    y_h, z_h = 2 * z + 1 - y, 2 * (2 * z1 + 1 - z0) + y

    def load(k, source, buf, sem):
        return pltpu.make_async_copy(source.at[pl.ds(k * rows, rows)], buf.at[k], sem.at[k])

    def load_weight(n):
        start = jnp.where(n < nt, (1 - y) * half + n * tile, y * half + (n - nt) * tile)
        columns = pl.ds(pl.multiple_of(start, tile), tile)
        return pltpu.make_async_copy(weight.at[:, columns], wbuf.at[n], wsem.at[n])

    def remote(src, dst, send, recv, tok, hid):
        return pltpu.make_async_remote_copy(
            src_ref=src, dst_ref=dst, send_sem=send, recv_sem=recv,
            device_id=(tok, hid), device_id_type=MESH,
        )

    def own(k, core):
        return hown.at[pl.ds(pl.multiple_of(core * tokens + k * rows, rows), rows)]

    def rem(k, core):
        return hrem.at[k, pl.ds(pl.multiple_of(core * rows, rows), rows)]

    def core_copy(k, core):
        return remote(own(k, core), own(k, core), cs.at[k], cr.at[k], core_t, h)

    def x_copy(k):
        return remote(own(k, c), rem(k, c), xs.at[k], xr.at[k], x_t, h)

    def relay(k, core):
        return remote(rem(k, core), rem(k, core), ls.at[k], lr.at[k], core_t, h)

    class Own:
        index, acc = nk, acc_o
        ysend, yrecv, zsend, zrecv, fsend = ysend_o, yrecv_o, zsend_o, zrecv_o, fsend_o
        chip, first, count = x, 0, tokens

        def hidden():
            return hown[...]

    def remote_chunk(k):
        class Rem:
            index, acc = k, acc_r.at[k]
            ysend, yrecv, zsend = ysend_r.at[k], yrecv_r.at[k], zsend_r.at[k]
            zrecv, fsend = zrecv_r.at[k], fsend_r.at[k]
            chip, first, count = 1 - x, pl.multiple_of(k * rows, rows), rows

            def hidden():
                return hrem[k]

        return Rem

    def y_copy(g, n):
        i = g.index
        return remote(g.ysend.at[n], g.yrecv.at[n], ys.at[i, n], yr.at[i, n], t, y_h)

    def z_copy(g, n):
        i = g.index
        return remote(g.zsend.at[n], g.zrecv.at[n], zs.at[i, n], zr.at[i, n], t, z_h)

    def final_copy(g, n, core, slot, tok):
        return remote(
            g.fsend.at[n, pl.ds(core * g.count, g.count)],
            land.at[slot, n, pl.ds(g.first, g.count)],
            fs.at[g.index, n, core], fr.at[slot, g.index, n], tok, 2 * t + y,
        )

    def each(count, step):
        def one(n, _):
            step(n)
            return 0

        lax.fori_loop(0, count, one, 0)

    for k in range(nk):
        load(k, gate, gbuf, gsem).start()
        load(k, up, ubuf, usem).start()
    for n in range(2 * nt):
        load_weight(n).start()

    barrier = pltpu.get_barrier_semaphore()

    def greet(tok, hid):
        pl.semaphore_signal(barrier, inc=1, device_id=(tok, hid), device_id_type=MESH)

    greet(core_t, h)
    greet(x_t, h)
    greet(t, y_h)

    @pl.when(gathers)
    def _():
        greet(t, z_h)

    source_h = [2 * (2 * slot + z0) + y for slot in range(2)]
    foreign = [jnp.logical_or(z != t, z1 != slot) for slot in range(2)]
    for slot in range(2):

        @pl.when(foreign[slot])
        def _():
            greet(z, source_h[slot])

    owners = jnp.where(z == t, 3, 4)
    pl.semaphore_wait(barrier, 3 + jnp.where(gathers, owners, 1))

    wide = 512

    def activate(k):
        load(k, gate, gbuf, gsem).wait()
        load(k, up, ubuf, usem).wait()

        def piece(j):
            columns = pl.ds(pl.multiple_of(j * wide, wide), wide)
            v = gbuf[k, :, columns].astype(F32)
            u = ubuf[k, :, columns].astype(F32)
            own(k, c)[:, columns] = (v / (1.0 + jnp.exp(-v)) * u).astype(BF16)

        each(ff // wide, piece)
        x_copy(k).start()
        core_copy(k, c).start()

    each(nk, activate)

    def multiply(g, first_use):
        def give(n):
            if first_use:
                load_weight(n).wait()
            g.ysend[n] = jnp.dot(g.hidden(), wbuf[n], preferred_element_type=F32).astype(BF16)
            y_copy(g, n).start()

        def keep(n):
            if first_use:
                load_weight(nt + n).wait()
            g.acc[n] = jnp.dot(g.hidden(), wbuf[nt + n], preferred_element_type=F32)

        each(nt, give)
        each(nt, keep)

    def after_y(g, n):
        y_copy(g, n).wait_recv()

        @pl.when(gathers)
        def _():
            g.acc[n] = g.acc[n] + g.yrecv[n].astype(F32)

        @pl.when(passes)
        def _():
            g.zsend[n] = (g.acc[n] + g.yrecv[n].astype(F32)).astype(BF16)
            z_copy(g, n).start()

    def is_local(g, core):
        tok = 2 * g.chip + core
        return tok, jnp.logical_and(tok == t, z == t)

    def after_z(g, n):
        @pl.when(gathers)
        def _():
            z_copy(g, n).wait_recv()
            g.fsend[n] = (g.acc[n] + g.zrecv[n].astype(F32)).astype(BF16)
            for core in range(2):
                tok, local = is_local(g, core)
                if g is Own:

                    @pl.when(local)
                    def _():
                        land[z1, n] = g.fsend[n, core * tokens : (core + 1) * tokens]

                    @pl.when(jnp.logical_not(local))
                    def _():
                        final_copy(g, n, core, z1, tok).start()

                else:
                    final_copy(g, n, core, z1, tok).start()

    for k in range(nk):
        core_copy(k, 1 - c).wait_recv()
    multiply(Own, True)
    after_y(Own, 0)

    def chunk(i):
        @pl.when(i < nk)
        def _():
            x_copy(i).wait_recv()
            relay(i, c).start()
            relay(i, 1 - c).wait_recv()
            multiply(remote_chunk(i), False)

        @pl.when(i + 1 < nt)
        def _():
            after_y(Own, i + 1)

        @pl.when(i < nt)
        def _():
            after_z(Own, i)

        @pl.when(jnp.logical_and(i >= 1, i <= nk))
        def _():
            g = remote_chunk(i - 1)
            each(nt, lambda n: after_y(g, n))

        @pl.when(i >= 2)
        def _():
            g = remote_chunk(i - 2)
            each(nt, lambda n: after_z(g, n))

    each(max(nk + 2, nt), chunk)

    def finish(first, count, index):
        for n in range(nt):
            for slot in range(2):

                @pl.when(foreign[slot])
                def _():
                    piece = land.at[slot, n, pl.ds(first, count)]
                    arrival = fr.at[slot, index, n]
                    remote(piece, piece, fs.at[0, 0, 0], arrival, core_t, h).wait_recv()

            out[pl.ds(first, count), n * tile : (n + 1) * tile] = land[
                0, n, pl.ds(first, count)
            ].astype(F32) + land[1, n, pl.ds(first, count)].astype(F32)

    @pl.when(z1 == x)
    def _():
        finish(0, tokens, nk)

    @pl.when(z1 != x)
    def _():
        each(nk, lambda k: finish(pl.multiple_of(k * rows, rows), rows, k))

    def drain_k(k):
        x_copy(k).wait_send()
        core_copy(k, c).wait_send()
        relay(k, c).wait_send()

    each(nk, drain_k)

    def drain(g):
        def step(n):
            y_copy(g, n).wait_send()

            @pl.when(passes)
            def _():
                z_copy(g, n).wait_send()

            @pl.when(gathers)
            def _():
                for core in range(2):
                    tok, local = is_local(g, core)

                    @pl.when(jnp.logical_not(local))
                    def _():
                        final_copy(g, n, core, z1, tok).wait_send()

        each(nt, step)

    drain(Own)
    each(nk, lambda k: drain(remote_chunk(k)))


def kernel_form(gate_pre, up_pre, down_weight, residual):
    tokens, ff = gate_pre.shape
    half = residual.shape[1]
    rows, nk, nt = ROWS, tokens // ROWS, half // TILE
    dma = pltpu.SemaphoreType.DMA
    summed = pl.pallas_call(
        kernel,
        out_shape=jax.ShapeDtypeStruct((tokens, half), F32),
        in_specs=[pl.BlockSpec(memory_space=pl.ANY)] * 3,
        out_specs=pl.BlockSpec(memory_space=pltpu.VMEM),
        scratch_shapes=[
            pltpu.VMEM((nk, rows, ff), BF16),
            pltpu.VMEM((nk, rows, ff), BF16),
            pltpu.VMEM((2 * nt, ff, TILE), BF16),
            pltpu.VMEM((2 * tokens, ff), BF16),
            pltpu.VMEM((nk, 2 * rows, ff), BF16),
            pltpu.VMEM((nt, 2 * tokens, TILE), F32),
        ]
        + [pltpu.VMEM((nt, 2 * tokens, TILE), BF16)] * 5
        + [pltpu.VMEM((nk, nt, 2 * rows, TILE), F32)]
        + [pltpu.VMEM((nk, nt, 2 * rows, TILE), BF16)] * 5
        + [pltpu.VMEM((2, nt, tokens, TILE), BF16)]
        + [dma((nk,)), dma((nk,)), dma((2 * nt,))]
        + [dma((nk,))] * 6
        + [dma((nk + 1, nt))] * 4
        + [dma((nk + 1, nt, 2)), dma((2, nk + 1, nt))],
        compiler_params=pltpu.CompilerParams(
            collective_id=0, has_side_effects=True, vmem_limit_bytes=50 * 2**20
        ),
        cost_estimate=pl.CostEstimate(
            flops=2 * 4 * tokens * ff * 2 * half,
            bytes_accessed=2 * ff * (2 * half + 2 * tokens),
            transcendentals=tokens * ff,
        ),
    )(gate_pre, up_pre, down_weight)
    return (summed + residual.astype(F32)).astype(BF16)


def solution(mesh):
    in_specs = (P("tok", "hid"), P("tok", "hid"), P("hid", "tok"), P("tok", "hid"))
    out_specs = P("tok", "hid")
    fits = mesh.shape["tok"] == 4 and mesh.shape["hid"] == 8
    return jax.shard_map(
        kernel_form if fits else collective_form,
        mesh=mesh, in_specs=in_specs, out_specs=out_specs, check_vma=False,
    )
```
